32 devices in a mesh: frame: 2 (over x), bx: 4 (over y, core), by: 4 (over z).
Axes of the slice: x: 2, y: 2, z: 4, core: 2. Of those that a mesh axis runs over, the one named last changes fastest.
Arguments:
- features: bfloat16 [8, 16, 64, 32, 512], P('frame', None, None, 'bx', 'by'), may hold values from -26 to 26
- voxel_embed: bfloat16 [16, 64, 32, 512], P(None, None, 'bx', 'by'), may hold values from -26 to 26
- visible: int32 [8, 16, 32, 512], P('frame', None, 'bx', 'by'), may hold values from 0 to 1, as said below
- w_query: bfloat16 [64, 64], replicated, may hold values from -0.75 to 0.75
- w_key: bfloat16 [64, 64], replicated, may hold values from -0.75 to 0.75
- w_value: bfloat16 [64, 64], replicated, may hold values from -0.75 to 0.75
- w_out: bfloat16 [64, 64], replicated, may hold values from -0.75 to 0.75
- conv_weight: bfloat16 [4, 3, 3, 3, 64, 64], replicated, may hold values from -0.21875 to 0.21875
- conv_bias: float32 [4, 64], replicated, may hold values from -1.2 to 1.2
Outputs:
- volume: bfloat16 [16, 64, 32, 512], P('frame', None, 'bx', 'by')
The draws below stay inside these ranges and needn't reach their ends.
Inputs may be any that keep to these rules, and one draw needn't show every extreme that they name: Every voxel has visible = 1 in at least one of the 8 frames.
All inputs are finite; a program needn't handle non-finite values.
Results may differ from the reference program's by a relative error of at most 0.025.
Values may be sent and summed in bfloat16 or wider, within the bound.
A program may use at most 64 MiB of HBM per device.

```python
import math
import jax
import jax.numpy as jnp
from jax import lax

C = 64
FR_DEV = 4
NZ = 16
LAYERS = 4
FRAMES = 8
NX = 32
NY = 512
N_FRAME = 2


def shared_surface(key):
    base = jnp.clip(jax.random.normal(jax.random.fold_in(key, 11), (NZ, C, NX, NY), jnp.float32), -4.0, 4.0)
    return base


def shared_basis(key):
    return jnp.clip(jax.random.normal(jax.random.fold_in(key, 21), (C, C), jnp.float32), -4.0, 4.0) / C ** 0.5


def draw_features(key, part):
    base = shared_surface(key)
    noise = jnp.clip(jax.random.normal(jax.random.fold_in(key, 12), (FRAMES, NZ, C, NX, NY), jnp.float32), -4.0, 4.0)
    return (base[None] + noise).astype(jnp.bfloat16)


def draw_voxel_embed(key, part):
    base = shared_surface(key)
    noise = jnp.clip(jax.random.normal(jax.random.fold_in(key, 14), (NZ, C, NX, NY), jnp.float32), -4.0, 4.0)
    level = 0.5
    return (base + level * noise).astype(jnp.bfloat16)


def draw_visible(key, part):
    coins = jax.random.randint(jax.random.fold_in(key, 31), (FRAMES, NZ, NX, NY), 0, 4)
    forced = jax.random.randint(jax.random.fold_in(key, 32), (1, NZ, NX, NY), 0, FRAMES)
    frame_ids = jnp.arange(FRAMES, dtype=jnp.int32).reshape((FRAMES, 1, 1, 1))
    return jnp.where((coins != 0) | (frame_ids == forced), 1, 0).astype(jnp.int32)


def draw_w_query(key, part):
    extra = jnp.clip(jax.random.normal(jax.random.fold_in(key, 22), (C, C), jnp.float32), -4.0, 4.0) / C ** 0.5
    return jnp.clip(shared_basis(key) + 0.5 * extra, -0.75, 0.75).astype(jnp.bfloat16)


def draw_w_key(key, part):
    extra = jnp.clip(jax.random.normal(jax.random.fold_in(key, 23), (C, C), jnp.float32), -4.0, 4.0) / C ** 0.5
    return jnp.clip(shared_basis(key) + 0.5 * extra, -0.75, 0.75).astype(jnp.bfloat16)


def bell_draw(key, shape, scale, reach, held_as=jnp.bfloat16):
    values = scale * jax.random.normal(key, shape, jnp.float32)
    return jnp.clip(values, min=-reach, max=reach).astype(held_as)


def setup_inputs(seed: int = 0) -> dict:
    keys = jax.random.split(jax.random.key(seed), 10)
    return {
        "features": draw_features(jax.random.fold_in(keys[9], 71), 0),
        "voxel_embed": draw_voxel_embed(jax.random.fold_in(keys[9], 71), 0),
        "visible": draw_visible(jax.random.fold_in(keys[9], 71), 0),
        "w_query": draw_w_query(jax.random.fold_in(keys[9], 71), 0),
        "w_key": draw_w_key(jax.random.fold_in(keys[9], 71), 0),
        "w_value": bell_draw(keys[5], (C, C), C ** -0.5, 0.75),
        "w_out": bell_draw(keys[6], (C, C), C ** -0.5, 0.75),
        "conv_weight": bell_draw(keys[7], (LAYERS, 3, 3, 3, C, C), (27 * C // 2) ** -0.5, 0.21875),
        "conv_bias": bell_draw(keys[8], (LAYERS, C), 0.3, 1.2, jnp.float32),
    }


absent_score = -1e+30
conv_layout = ('NDCHW', 'DHWIO', 'NDCHW')

def group_partial(query_data, group_feats, group_seen, w_key, w_value):
    high = lax.Precision.HIGHEST
    as_float = group_feats.astype(jnp.float32)
    key_data = jnp.einsum('fzcxy,cd->fzdxy', as_float, w_key.astype(jnp.float32), precision=high).astype(jnp.bfloat16)
    value_data = jnp.einsum('fzcxy,cd->fzdxy', as_float, w_value.astype(jnp.float32), precision=high).astype(jnp.bfloat16)
    scores = jnp.einsum('zdxy,fzdxy->fzxy', query_data.astype(jnp.float32), key_data.astype(jnp.float32), precision=high) / math.sqrt(C)
    is_seen = group_seen > 0
    highest = lax.optimization_barrier(jnp.max(jnp.where(is_seen, scores, absent_score), axis=0))
    weights = jnp.where(is_seen, jnp.exp(scores - highest[None]), 0.0)
    weighted = lax.optimization_barrier(jnp.sum(weights[:, :, None] * value_data.astype(jnp.float32), axis=0)).astype(jnp.bfloat16)
    totals = lax.optimization_barrier(jnp.sum(weights, axis=0)).astype(jnp.bfloat16)
    return (highest, weighted, totals)

def reference(features, voxel_embed, visible, w_query, w_key, w_value, w_out, conv_weight, conv_bias):
    high = lax.Precision.HIGHEST
    query_data = jnp.einsum('zcxy,cd->zdxy', voxel_embed.astype(jnp.float32), w_query.astype(jnp.float32), precision=high).astype(jnp.bfloat16)
    grouped = features.reshape((N_FRAME, FR_DEV) + features.shape[1:])
    seen_groups = visible.reshape((N_FRAME, FR_DEV) + visible.shape[1:])
    highest, weighted, totals = lax.map(lambda pair: group_partial(query_data, pair[0], pair[1], w_key, w_value), (grouped, seen_groups))
    overall = lax.optimization_barrier(jnp.max(highest, axis=0))
    factor = jnp.exp(highest - overall[None])
    merged = lax.optimization_barrier(jnp.sum(factor[:, :, None] * weighted.astype(jnp.float32), axis=0))
    norm_sum = lax.optimization_barrier(jnp.sum(factor * totals.astype(jnp.float32), axis=0))
    attended = (merged / norm_sum[:, None]).astype(jnp.bfloat16)
    hidden = jnp.einsum('zcxy,cd->zdxy', attended.astype(jnp.float32), w_out.astype(jnp.float32), precision=high).astype(jnp.bfloat16)
    for layer_no in range(LAYERS):
        result = lax.conv_general_dilated(hidden[None].astype(jnp.float32), conv_weight[layer_no].astype(jnp.float32), (1, 1, 1), ((1, 1), (1, 1), (1, 1)), dimension_numbers=conv_layout, precision=high)[0]
        result = result + conv_bias[layer_no][None, :, None, None]
        if layer_no + 1 < LAYERS:
            result = jnp.maximum(result, 0.0)
        hidden = result.astype(jnp.bfloat16)
    return hidden
```

```python
import functools
import itertools
import math

import jax
import jax.numpy as jnp
from jax import lax
from jax.experimental import pallas as pl
from jax.experimental.pallas import tpu as pltpu
from jax.sharding import PartitionSpec as P

MESH = pl.DeviceIdType.MESH
absent_score = -1e30


def conv_kernel(
    sizes, layers, planes, rows, ch, cols, hid_ref, w_ref, b_ref, out_ref, s3, edge_out, edge_in, send_sem, recv_sem
):
    spots = [lax.axis_index(a) for a in ("frame", "bx", "by")]
    dirs = [
        d
        for d in itertools.product((-1, 0, 1), repeat=3)
        if any(d) and all(k == 0 or n > 1 for k, n in zip(d, sizes))
    ]

    def number(d):
        return (d[0] + 1) * 9 + (d[1] + 1) * 3 + d[2] + 1

    def beside(d):
        found = None
        for k, spot, n in zip(d, spots, sizes):
            if k:
                here = spot > 0 if k < 0 else spot < n - 1
                found = here if found is None else jnp.logical_and(found, here)
        return found

    def device(d):
        return tuple(spot + k for spot, k in zip(spots, d))

    def each(act):
        for d in dirs:
            pl.when(beside(d))(functools.partial(act, d))

    def source(k, length):
        return {-1: pl.ds(1, 1), 0: pl.ds(1, length), 1: pl.ds(length, 1)}[k]

    def halo(k, length):
        return {-1: pl.ds(0, 1), 0: pl.ds(1, length), 1: pl.ds(length + 1, 1)}[k]

    def landing(p, d):
        if d[2] == 0:
            return s3.at[p, halo(d[0], planes), halo(d[1], rows), 1]
        return edge_in.at[p, 0 if d[2] < 0 else 1, d[0] + 1, d[1] + 1]

    def outgoing(p, d):
        if d[2] == 0:
            src = s3.at[p, source(d[0], planes), source(d[1], rows), 1]
        else:
            src = edge_out.at[0 if d[2] < 0 else 1]
        back = tuple(-k for k in d)
        return pltpu.make_async_remote_copy(
            src_ref=src,
            dst_ref=landing(p, back),
            send_sem=send_sem.at[number(d)],
            recv_sem=recv_sem.at[p, number(back)],
            device_id=device(d),
            device_id_type=MESH,
        )

    def incoming(p, d):
        return pltpu.make_async_remote_copy(
            src_ref=landing(p, d),
            dst_ref=landing(p, d),
            send_sem=send_sem.at[number(d)],
            recv_sem=recv_sem.at[p, number(d)],
            device_id=device(d),
            device_id_type=MESH,
        )

    zero = jnp.zeros((ch, cols), jnp.bfloat16)
    for p in range(2):
        for x in range(rows + 2):
            s3[p, 0, x, 1] = zero
            s3[p, planes + 1, x, 1] = zero
        for z in range(1, planes + 1):
            s3[p, z, 0, 1] = zero
            s3[p, z, rows + 1, 1] = zero
        edge_in[p] = jnp.zeros(edge_in.shape[1:], jnp.bfloat16)
    for z in range(planes):
        for x in range(rows):
            s3[0, z + 1, x + 1, 1] = hid_ref[z, x]

    barrier = pltpu.get_barrier_semaphore()
    each(lambda d: pl.semaphore_signal(barrier, inc=1, device_id=device(d), device_id_type=MESH))
    peers = 1
    for spot, n in zip(spots, sizes):
        peers = peers * (1 + (spot > 0).astype(jnp.int32) + (spot < n - 1).astype(jnp.int32))
    pl.semaphore_wait(barrier, peers - 1)

    lane = lax.broadcasted_iota(jnp.int32, (ch, cols), 1)
    pair = 2 if rows % 2 == 0 else 1

    def layer(l, carry):
        p = lax.rem(l, 2)

        def pack(z, held):
            low, high = held
            for x in range(rows):
                v = s3[p, z + 1, x + 1, 1].astype(jnp.float32)
                j = z * rows + x
                low = jnp.where(lane == j, pltpu.roll(v, j, 1), low)
                high = jnp.where(lane == j, pltpu.roll(v, lax.rem(j + 1, cols), 1), high)
            return low, high

        blank = jnp.zeros((ch, cols), jnp.float32)
        low, high = lax.fori_loop(0, planes, pack, (blank, blank))
        edge_out[0] = low.astype(jnp.bfloat16)
        edge_out[1] = high.astype(jnp.bfloat16)
        each(lambda d: outgoing(p, d).start())
        each(lambda d: incoming(p, d).wait_recv())

        def shift(zp, c):
            dz = (zp + planes - 1) // planes
            z = lax.rem(zp + planes - 1, planes)
            for xp in range(rows + 2):
                dx, x = (xp + rows - 1) // rows, (xp + rows - 1) % rows
                j = z * rows + x
                v = s3[p, zp, xp, 1].astype(jnp.float32)
                before = edge_in[p, 0, dz, dx].astype(jnp.float32)
                after = edge_in[p, 1, dz, dx].astype(jnp.float32)
                left = jnp.where(lane == 0, pltpu.roll(before, lax.rem(cols - j, cols), 1), pltpu.roll(v, 1, 1))
                right = jnp.where(
                    lane == cols - 1, pltpu.roll(after, cols - 1 - j, 1), pltpu.roll(v, cols - 1, 1)
                )
                s3[p, zp, xp, 0] = left.astype(jnp.bfloat16)
                s3[p, zp, xp, 2] = right.astype(jnp.bfloat16)
            return c

        lax.fori_loop(0, planes + 2, shift, 0)

        bias = b_ref[l]

        def strip(i, c):
            x0 = i * pair
            sums = {}
            for zp in range(planes + 2):
                lo, hi = max(0, zp - planes + 1), min(2, zp)
                taps = [s3[p, zp, pl.ds(x0 + k, 3)].reshape(9 * ch, cols) for k in range(pair)]
                data = jnp.concatenate(taps, axis=1) if pair > 1 else taps[0]
                part = jnp.dot(w_ref[l, lo * ch : (hi + 1) * ch], data, preferred_element_type=jnp.float32)
                for a in range(lo, hi + 1):
                    term = part[(a - lo) * ch : (a - lo + 1) * ch]
                    z = zp - a
                    sums[z] = sums[z] + term if z in sums else term
                z = zp - 2
                if z >= 0:
                    h = sums.pop(z) + bias
                    h = jnp.where(l < layers - 1, jnp.maximum(h, 0.0), h).astype(jnp.bfloat16)
                    for k in range(pair):
                        s3[1 - p, z + 1, x0 + 1 + k, 1] = h[:, k * cols : (k + 1) * cols]
            return c

        lax.fori_loop(0, rows // pair, strip, 0)
        each(lambda d: outgoing(p, d).wait_send())
        return carry

    lax.fori_loop(0, layers, layer, 0)
    for z in range(planes):
        for x in range(rows):
            out_ref[z, x] = s3[layers % 2, z + 1, x + 1, 1]


def convs(sizes, hidden, conv_weight, conv_bias):
    planes, rows, ch, cols = hidden.shape
    layers = conv_weight.shape[0]
    w = conv_weight.transpose(0, 1, 5, 2, 3, 4).reshape(layers, 3 * ch, 9 * ch)
    whole = pl.BlockSpec(memory_space=pltpu.VMEM)
    return pl.pallas_call(
        functools.partial(conv_kernel, sizes, layers, planes, rows, ch, cols),
        out_shape=jax.ShapeDtypeStruct(hidden.shape, jnp.bfloat16),
        in_specs=[whole] * 3,
        out_specs=whole,
        scratch_shapes=[
            pltpu.VMEM((2, planes + 2, rows + 2, 3, ch, cols), jnp.bfloat16),
            pltpu.VMEM((2, ch, cols), jnp.bfloat16),
            pltpu.VMEM((2, 2, 3, 3, ch, cols), jnp.bfloat16),
            pltpu.SemaphoreType.DMA((27,)),
            pltpu.SemaphoreType.DMA((2, 27)),
        ],
        compiler_params=pltpu.CompilerParams(
            collective_id=1, has_side_effects=True, vmem_limit_bytes=40 * 1024 * 1024
        ),
    )(hidden, w, conv_bias[:, :, None])


def shards(sizes, features, voxel_embed, visible, w_query, w_key, w_value, w_out, conv_weight, conv_bias):
    width = w_key.shape[0]
    query_data = jnp.einsum(
        "zcxy,cd->zdxy", voxel_embed, w_query, preferred_element_type=jnp.float32
    ).astype(jnp.bfloat16)
    key_data = jnp.einsum(
        "fzcxy,cd->fzdxy", features, w_key, preferred_element_type=jnp.float32
    ).astype(jnp.bfloat16)
    value_data = jnp.einsum(
        "fzcxy,cd->fzdxy", features, w_value, preferred_element_type=jnp.float32
    ).astype(jnp.bfloat16)
    scores = jnp.einsum(
        "zdxy,fzdxy->fzxy", query_data, key_data, preferred_element_type=jnp.float32
    ) / math.sqrt(width)
    is_seen = visible > 0
    highest = jnp.max(jnp.where(is_seen, scores, absent_score), axis=0)
    weights = jnp.where(is_seen, jnp.exp(scores - highest[None]), 0.0)
    weighted = jnp.sum(weights[:, :, None] * value_data, axis=0).astype(jnp.bfloat16)
    totals = jnp.sum(weights, axis=0).astype(jnp.bfloat16)
    groups = lax.axis_size("frame")
    got_weighted, got_totals = (
        lax.all_to_all(weighted, "frame", split_axis=0, concat_axis=0, tiled=True),
        lax.all_to_all(totals, "frame", split_axis=0, concat_axis=0, tiled=True),
    )
    got_highest = lax.all_to_all(
        highest.astype(jnp.bfloat16), "frame", split_axis=0, concat_axis=0, tiled=True
    ).astype(highest.dtype)
    planes = got_highest.shape[0] // groups
    got_weighted = got_weighted.reshape((groups, planes) + got_weighted.shape[1:])
    got_totals = got_totals.reshape((groups, planes) + got_totals.shape[1:])
    got_highest = got_highest.reshape((groups, planes) + got_highest.shape[1:])
    overall = jnp.max(got_highest, axis=0)
    factor = jnp.exp(got_highest - overall[None])
    merged = jnp.sum(factor[:, :, None] * got_weighted.astype(jnp.float32), axis=0)
    norm_sum = jnp.sum(factor * got_totals.astype(jnp.float32), axis=0)
    attended = (merged / norm_sum[:, None]).astype(jnp.bfloat16)
    hidden = jnp.einsum(
        "zcxy,cd->zxdy", attended, w_out, preferred_element_type=jnp.float32
    ).astype(jnp.bfloat16)
    return convs(sizes, hidden, conv_weight, conv_bias).transpose(0, 2, 1, 3)


def solution(mesh):
    sizes = tuple(mesh.shape[a] for a in ("frame", "bx", "by"))
    return jax.shard_map(
        functools.partial(shards, sizes),
        mesh=mesh,
        in_specs=(
            P("frame", None, None, "bx", "by"),
            P(None, None, "bx", "by"),
            P("frame", None, "bx", "by"),
            P(),
            P(),
            P(),
            P(),
            P(),
            P(),
        ),
        out_specs=P("frame", None, "bx", "by"),
        check_vma=False,
    )
```

```python
import functools
import itertools
import math

import jax
import jax.numpy as jnp
from jax import lax
from jax.experimental import pallas as pl
from jax.experimental.pallas import tpu as pltpu
from jax.sharding import PartitionSpec as P

MESH = pl.DeviceIdType.MESH
absent_score = -1e30


def conv_kernel(
    sizes, layers, planes, rows, ch, cols, hid_ref, w_ref, b_ref, out_ref, s3, edge_out, edge_in, send_sem, recv_sem
):
    spots = [lax.axis_index(a) for a in ("frame", "bx", "by")]
    dirs = [
        d
        for d in itertools.product((-1, 0, 1), repeat=3)
        if any(d) and all(k == 0 or n > 1 for k, n in zip(d, sizes))
    ]

    def number(d):
        return (d[0] + 1) * 9 + (d[1] + 1) * 3 + d[2] + 1

    def beside(d):
        found = None
        for k, spot, n in zip(d, spots, sizes):
            if k:
                here = spot > 0 if k < 0 else spot < n - 1
                found = here if found is None else jnp.logical_and(found, here)
        return found

    def device(d):
        return tuple(spot + k for spot, k in zip(spots, d))

    def each(act, some=lambda d: True):
        for d in filter(some, dirs):
            pl.when(beside(d))(functools.partial(act, d))

    def flat(d):
        return d[2] == 0

    def column(d):
        return d[2] != 0

    def straight(d):
        return d[:2] == (0, 0)

    def source(k, length):
        return {-1: pl.ds(1, 1), 0: pl.ds(1, length), 1: pl.ds(length, 1)}[k]

    def halo(k, length):
        return {-1: pl.ds(0, 1), 0: pl.ds(1, length), 1: pl.ds(length + 1, 1)}[k]

    def landing(p, d):
        if d[2] == 0:
            return s3.at[p, halo(d[0], planes), halo(d[1], rows), 1]
        return edge_in.at[p, 0 if d[2] < 0 else 1, d[0] + 1, d[1] + 1]

    def outgoing(p, d):
        if d[2] == 0:
            src = s3.at[p, source(d[0], planes), source(d[1], rows), 1]
        else:
            src = edge_out.at[0 if d[2] < 0 else 1]
        back = tuple(-k for k in d)
        return pltpu.make_async_remote_copy(
            src_ref=src,
            dst_ref=landing(p, back),
            send_sem=send_sem.at[number(d)],
            recv_sem=recv_sem.at[p, number(back)],
            device_id=device(d),
            device_id_type=MESH,
        )

    def incoming(p, d):
        return pltpu.make_async_remote_copy(
            src_ref=landing(p, d),
            dst_ref=landing(p, d),
            send_sem=send_sem.at[number(d)],
            recv_sem=recv_sem.at[p, number(d)],
            device_id=device(d),
            device_id_type=MESH,
        )

    zero = jnp.zeros((ch, cols), jnp.bfloat16)
    for p in range(2):
        for x in range(rows + 2):
            s3[p, 0, x, 1] = zero
            s3[p, planes + 1, x, 1] = zero
        for z in range(1, planes + 1):
            s3[p, z, 0, 1] = zero
            s3[p, z, rows + 1, 1] = zero
        edge_in[p] = jnp.zeros(edge_in.shape[1:], jnp.bfloat16)
    for z in range(planes):
        for x in range(rows):
            s3[0, z + 1, x + 1, 1] = hid_ref[z, x]

    barrier = pltpu.get_barrier_semaphore()
    each(lambda d: pl.semaphore_signal(barrier, inc=1, device_id=device(d), device_id_type=MESH))
    peers = 1
    for spot, n in zip(spots, sizes):
        peers = peers * (1 + (spot > 0).astype(jnp.int32) + (spot < n - 1).astype(jnp.int32))
    pl.semaphore_wait(barrier, peers - 1)

    lane = lax.broadcasted_iota(jnp.int32, (ch, cols), 1)
    pair = 2 if rows % 2 == 0 else 1

    def layer(l, carry):
        p = lax.rem(l, 2)

        def pack(z, held):
            low, high = held
            for x in range(rows):
                v = s3[p, z + 1, x + 1, 1].astype(jnp.float32)
                j = z * rows + x
                low = jnp.where(lane == j, pltpu.roll(v, j, 1), low)
                high = jnp.where(lane == j, pltpu.roll(v, lax.rem(j + 1, cols), 1), high)
            return low, high

        each(lambda d: outgoing(p, d).start(), flat)
        blank = jnp.zeros((ch, cols), jnp.float32)
        low, high = lax.fori_loop(0, planes, pack, (blank, blank))
        edge_out[0] = low.astype(jnp.bfloat16)
        edge_out[1] = high.astype(jnp.bfloat16)
        each(lambda d: outgoing(p, d).start(), straight)
        each(lambda d: outgoing(p, d).start(), lambda d: column(d) and not straight(d))

        def shift(xps, zp, c):
            dz = (zp + planes - 1) // planes
            z = lax.rem(zp + planes - 1, planes)
            for xp in xps:
                dx, x = (xp + rows - 1) // rows, (xp + rows - 1) % rows
                j = z * rows + x
                v = s3[p, zp, xp, 1].astype(jnp.float32)
                before = edge_in[p, 0, dz, dx].astype(jnp.float32)
                after = edge_in[p, 1, dz, dx].astype(jnp.float32)
                left = jnp.where(lane == 0, pltpu.roll(before, lax.rem(cols - j, cols), 1), pltpu.roll(v, 1, 1))
                right = jnp.where(
                    lane == cols - 1, pltpu.roll(after, cols - 1 - j, 1), pltpu.roll(v, cols - 1, 1)
                )
                s3[p, zp, xp, 0] = left.astype(jnp.bfloat16)
                s3[p, zp, xp, 2] = right.astype(jnp.bfloat16)
            return c

        each(lambda d: incoming(p, d).wait_recv(), straight)
        lax.fori_loop(1, planes + 1, functools.partial(shift, range(1, rows + 1)), 0)
        each(lambda d: incoming(p, d).wait_recv(), lambda d: not straight(d))
        lax.fori_loop(1, planes + 1, functools.partial(shift, (0, rows + 1)), 0)
        lax.fori_loop(0, 2, lambda k, c: shift(range(rows + 2), k * (planes + 1), c), 0)

        bias = b_ref[l]

        def strip(i, c):
            x0 = i * pair
            sums = {}
            for zp in range(planes + 2):
                lo, hi = max(0, zp - planes + 1), min(2, zp)
                taps = [s3[p, zp, pl.ds(x0 + k, 3)].reshape(9 * ch, cols) for k in range(pair)]
                data = jnp.concatenate(taps, axis=1) if pair > 1 else taps[0]
                part = jnp.dot(w_ref[l, lo * ch : (hi + 1) * ch], data, preferred_element_type=jnp.float32)
                for a in range(lo, hi + 1):
                    term = part[(a - lo) * ch : (a - lo + 1) * ch]
                    z = zp - a
                    sums[z] = sums[z] + term if z in sums else term
                z = zp - 2
                if z >= 0:
                    h = sums.pop(z) + bias
                    h = jnp.where(l < layers - 1, jnp.maximum(h, 0.0), h).astype(jnp.bfloat16)
                    for k in range(pair):
                        s3[1 - p, z + 1, x0 + 1 + k, 1] = h[:, k * cols : (k + 1) * cols]
            return c

        lax.fori_loop(0, rows // pair, strip, 0)
        each(lambda d: outgoing(p, d).wait_send())
        return carry

    lax.fori_loop(0, layers, layer, 0)
    for z in range(planes):
        for x in range(rows):
            out_ref[z, x] = s3[layers % 2, z + 1, x + 1, 1]


def convs(sizes, hidden, conv_weight, conv_bias):
    planes, rows, ch, cols = hidden.shape
    layers = conv_weight.shape[0]
    w = conv_weight.transpose(0, 1, 5, 2, 3, 4).reshape(layers, 3 * ch, 9 * ch)
    whole = pl.BlockSpec(memory_space=pltpu.VMEM)
    return pl.pallas_call(
        functools.partial(conv_kernel, sizes, layers, planes, rows, ch, cols),
        out_shape=jax.ShapeDtypeStruct(hidden.shape, jnp.bfloat16),
        in_specs=[whole] * 3,
        out_specs=whole,
        scratch_shapes=[
            pltpu.VMEM((2, planes + 2, rows + 2, 3, ch, cols), jnp.bfloat16),
            pltpu.VMEM((2, ch, cols), jnp.bfloat16),
            pltpu.VMEM((2, 2, 3, 3, ch, cols), jnp.bfloat16),
            pltpu.SemaphoreType.DMA((27,)),
            pltpu.SemaphoreType.DMA((2, 27)),
        ],
        compiler_params=pltpu.CompilerParams(
            collective_id=1, has_side_effects=True, vmem_limit_bytes=40 * 1024 * 1024
        ),
    )(hidden, w, conv_bias[:, :, None])


def shards(sizes, features, voxel_embed, visible, w_query, w_key, w_value, w_out, conv_weight, conv_bias):
    width = w_key.shape[0]
    query_data = jnp.einsum(
        "zcxy,cd->zdxy", voxel_embed, w_query, preferred_element_type=jnp.float32
    ).astype(jnp.bfloat16)
    key_data = jnp.einsum(
        "fzcxy,cd->fzdxy", features, w_key, preferred_element_type=jnp.float32
    ).astype(jnp.bfloat16)
    value_data = jnp.einsum(
        "fzcxy,cd->fzdxy", features, w_value, preferred_element_type=jnp.float32
    ).astype(jnp.bfloat16)
    scores = jnp.einsum(
        "zdxy,fzdxy->fzxy", query_data, key_data, preferred_element_type=jnp.float32
    ) / math.sqrt(width)
    is_seen = visible > 0
    highest = jnp.max(jnp.where(is_seen, scores, absent_score), axis=0)
    weights = jnp.where(is_seen, jnp.exp(scores - highest[None]), 0.0)
    weighted = jnp.sum(weights[:, :, None] * value_data, axis=0).astype(jnp.bfloat16)
    totals = jnp.sum(weights, axis=0).astype(jnp.bfloat16)
    groups = lax.axis_size("frame")
    sent = jnp.concatenate([weighted, totals[:, None], highest.astype(jnp.bfloat16)[:, None]], axis=1)
    got = lax.all_to_all(sent, "frame", split_axis=0, concat_axis=0, tiled=True)
    got = got.reshape((groups, got.shape[0] // groups) + got.shape[1:])
    got_weighted, got_totals = got[:, :, :width], got[:, :, width]
    got_highest = got[:, :, width + 1].astype(jnp.float32)
    overall = jnp.max(got_highest, axis=0)
    factor = jnp.exp(got_highest - overall[None])
    merged = jnp.sum(factor[:, :, None] * got_weighted.astype(jnp.float32), axis=0)
    norm_sum = jnp.sum(factor * got_totals.astype(jnp.float32), axis=0)
    attended = (merged / norm_sum[:, None]).astype(jnp.bfloat16)
    hidden = jnp.einsum(
        "zcxy,cd->zxdy", attended, w_out, preferred_element_type=jnp.float32
    ).astype(jnp.bfloat16)
    return convs(sizes, hidden, conv_weight, conv_bias).transpose(0, 2, 1, 3)


def solution(mesh):
    sizes = tuple(mesh.shape[a] for a in ("frame", "bx", "by"))
    return jax.shard_map(
        functools.partial(shards, sizes),
        mesh=mesh,
        in_specs=(
            P("frame", None, None, "bx", "by"),
            P(None, None, "bx", "by"),
            P("frame", None, "bx", "by"),
            P(),
            P(),
            P(),
            P(),
            P(),
            P(),
        ),
        out_specs=P("frame", None, "bx", "by"),
        check_vma=False,
    )
```

```python
import functools
import itertools
import math

import jax
import jax.numpy as jnp
from jax import lax
from jax.experimental import pallas as pl
from jax.experimental.pallas import tpu as pltpu
from jax.sharding import PartitionSpec as P

MESH = pl.DeviceIdType.MESH
absent_score = -1e30


def conv_kernel(
    sizes, layers, planes, rows, ch, cols, hid_ref, w_ref, b_ref, out_ref, s3, edge_out, edge_in, partial_sums, send_sem, recv_sem
):
    spots = [lax.axis_index(a) for a in ("frame", "bx", "by")]
    dirs = [
        d
        for d in itertools.product((-1, 0, 1), repeat=3)
        if any(d) and all(k == 0 or n > 1 for k, n in zip(d, sizes))
    ]

    def number(d):
        return (d[0] + 1) * 9 + (d[1] + 1) * 3 + d[2] + 1

    def beside(d):
        found = None
        for k, spot, n in zip(d, spots, sizes):
            if k:
                here = spot > 0 if k < 0 else spot < n - 1
                found = here if found is None else jnp.logical_and(found, here)
        return found

    def device(d):
        return tuple(spot + k for spot, k in zip(spots, d))

    def each(act, some=lambda d: True):
        for d in filter(some, dirs):
            pl.when(beside(d))(functools.partial(act, d))

    def flat(d):
        return d[2] == 0

    def column(d):
        return d[2] != 0

    def straight(d):
        return d[:2] == (0, 0)

    def source(k, length):
        return {-1: pl.ds(1, 1), 0: pl.ds(1, length), 1: pl.ds(length, 1)}[k]

    def halo(k, length):
        return {-1: pl.ds(0, 1), 0: pl.ds(1, length), 1: pl.ds(length + 1, 1)}[k]

    def landing(p, d):
        if d[2] == 0:
            return s3.at[p, halo(d[0], planes), halo(d[1], rows), 1]
        return edge_in.at[p, 0 if d[2] < 0 else 1, d[0] + 1, d[1] + 1]

    def outgoing(p, d):
        if d[2] == 0:
            src = s3.at[p, source(d[0], planes), source(d[1], rows), 1]
        else:
            src = edge_out.at[0 if d[2] < 0 else 1]
        back = tuple(-k for k in d)
        return pltpu.make_async_remote_copy(
            src_ref=src,
            dst_ref=landing(p, back),
            send_sem=send_sem.at[number(d)],
            recv_sem=recv_sem.at[p, number(back)],
            device_id=device(d),
            device_id_type=MESH,
        )

    def incoming(p, d):
        return pltpu.make_async_remote_copy(
            src_ref=landing(p, d),
            dst_ref=landing(p, d),
            send_sem=send_sem.at[number(d)],
            recv_sem=recv_sem.at[p, number(d)],
            device_id=device(d),
            device_id_type=MESH,
        )

    zero = jnp.zeros((ch, cols), jnp.bfloat16)
    for p in range(2):
        for x in range(rows + 2):
            s3[p, 0, x, 1] = zero
            s3[p, planes + 1, x, 1] = zero
        for z in range(1, planes + 1):
            s3[p, z, 0, 1] = zero
            s3[p, z, rows + 1, 1] = zero
        edge_in[p] = jnp.zeros(edge_in.shape[1:], jnp.bfloat16)
    for z in range(planes):
        for x in range(rows):
            s3[0, z + 1, x + 1, 1] = hid_ref[z, x]

    barrier = pltpu.get_barrier_semaphore()
    each(lambda d: pl.semaphore_signal(barrier, inc=1, device_id=device(d), device_id_type=MESH))
    peers = 1
    for spot, n in zip(spots, sizes):
        peers = peers * (1 + (spot > 0).astype(jnp.int32) + (spot < n - 1).astype(jnp.int32))
    pl.semaphore_wait(barrier, peers - 1)

    lane = lax.broadcasted_iota(jnp.int32, (ch, cols), 1)
    pair = 2 if rows % 2 == 0 else 1
    ends = sorted({0, planes - 1})

    def layer(l, carry):
        p = lax.rem(l, 2)

        def pack(z, held):
            low, high = held
            for x in range(rows):
                v = s3[p, z + 1, x + 1, 1].astype(jnp.float32)
                j = z * rows + x
                low = jnp.where(lane == j, pltpu.roll(v, j, 1), low)
                high = jnp.where(lane == j, pltpu.roll(v, lax.rem(j + 1, cols), 1), high)
            return low, high

        each(lambda d: outgoing(p, d).start(), flat)
        blank = jnp.zeros((ch, cols), jnp.float32)
        low, high = lax.fori_loop(0, planes, pack, (blank, blank))
        edge_out[0] = low.astype(jnp.bfloat16)
        edge_out[1] = high.astype(jnp.bfloat16)
        each(lambda d: outgoing(p, d).start(), straight)
        each(lambda d: outgoing(p, d).start(), lambda d: column(d) and not straight(d))

        def shift(xps, zp, c):
            dz = (zp + planes - 1) // planes
            z = lax.rem(zp + planes - 1, planes)
            for xp in xps:
                dx, x = (xp + rows - 1) // rows, (xp + rows - 1) % rows
                j = z * rows + x
                v = s3[p, zp, xp, 1].astype(jnp.float32)
                before = edge_in[p, 0, dz, dx].astype(jnp.float32)
                after = edge_in[p, 1, dz, dx].astype(jnp.float32)
                left = jnp.where(lane == 0, pltpu.roll(before, lax.rem(cols - j, cols), 1), pltpu.roll(v, 1, 1))
                right = jnp.where(
                    lane == cols - 1, pltpu.roll(after, cols - 1 - j, 1), pltpu.roll(v, cols - 1, 1)
                )
                s3[p, zp, xp, 0] = left.astype(jnp.bfloat16)
                s3[p, zp, xp, 2] = right.astype(jnp.bfloat16)
            return c

        each(lambda d: incoming(p, d).wait_recv(), straight)
        lax.fori_loop(1, planes + 1, functools.partial(shift, range(1, rows + 1)), 0)
        bias = b_ref[l]

        def product(x0, zp, lo, hi):
            taps = [s3[p, zp, pl.ds(x0 + k, 3)].reshape(9 * ch, cols) for k in range(pair)]
            data = jnp.concatenate(taps, axis=1) if pair > 1 else taps[0]
            return jnp.dot(w_ref[l, lo * ch : (hi + 1) * ch], data, preferred_element_type=jnp.float32)

        def finish(x0, z, total):
            h = total + bias
            h = jnp.where(l < layers - 1, jnp.maximum(h, 0.0), h).astype(jnp.bfloat16)
            for k in range(pair):
                s3[1 - p, z + 1, x0 + 1 + k, 1] = h[:, k * cols : (k + 1) * cols]

        def gather(x0, zps, sums):
            for zp in zps:
                lo, hi = max(0, zp - planes + 1), min(2, zp)
                part = product(x0, zp, lo, hi)
                for a in range(lo, hi + 1):
                    term = part[(a - lo) * ch : (a - lo + 1) * ch]
                    z = zp - a
                    sums[z] = sums[z] + term if z in sums else term
                if zp >= 2 and zp - 2 not in ends:
                    finish(x0, zp - 2, sums.pop(zp - 2))

        def inner_first(i, c):
            sums = {}
            gather(i * pair, range(1, planes + 1), sums)
            for n, z in enumerate(ends):
                partial_sums[i, n] = sums[z]
            return c

        def inner_last(i, c):
            x0 = i * pair
            for n, z in enumerate(ends):
                total = partial_sums[i, n]
                if z == 0:
                    total = total + product(x0, 0, 0, 0)
                if z == planes - 1:
                    total = total + product(x0, planes + 1, 2, 2)
                finish(x0, z, total)
            return c

        def outer(i, c):
            sums = {}
            gather(i * pair, range(planes + 2), sums)
            for z in ends:
                finish(i * pair, z, sums[z])
            return c

        strips = rows // pair
        lax.fori_loop(1, strips - 1, inner_first, 0)
        each(lambda d: incoming(p, d).wait_recv(), lambda d: not straight(d))
        lax.fori_loop(1, planes + 1, functools.partial(shift, (0, rows + 1)), 0)
        lax.fori_loop(0, 2, lambda k, c: shift(range(rows + 2), k * (planes + 1), c), 0)
        lax.fori_loop(1, strips - 1, inner_last, 0)
        edges = min(strips, 2)
        lax.fori_loop(0, edges, lambda k, c: outer(k * (strips - 1), c), 0)
        each(lambda d: outgoing(p, d).wait_send())
        return carry

    lax.fori_loop(0, layers, layer, 0)
    for z in range(planes):
        for x in range(rows):
            out_ref[z, x] = s3[layers % 2, z + 1, x + 1, 1]


def convs(sizes, hidden, conv_weight, conv_bias):
    planes, rows, ch, cols = hidden.shape
    layers = conv_weight.shape[0]
    w = conv_weight.transpose(0, 1, 5, 2, 3, 4).reshape(layers, 3 * ch, 9 * ch)
    whole = pl.BlockSpec(memory_space=pltpu.VMEM)
    return pl.pallas_call(
        functools.partial(conv_kernel, sizes, layers, planes, rows, ch, cols),
        out_shape=jax.ShapeDtypeStruct(hidden.shape, jnp.bfloat16),
        in_specs=[whole] * 3,
        out_specs=whole,
        scratch_shapes=[
            pltpu.VMEM((2, planes + 2, rows + 2, 3, ch, cols), jnp.bfloat16),
            pltpu.VMEM((2, ch, cols), jnp.bfloat16),
            pltpu.VMEM((2, 2, 3, 3, ch, cols), jnp.bfloat16),
            pltpu.VMEM((rows, 2, ch, 2 * cols if rows % 2 == 0 else cols), jnp.float32),
            pltpu.SemaphoreType.DMA((27,)),
            pltpu.SemaphoreType.DMA((2, 27)),
        ],
        compiler_params=pltpu.CompilerParams(
            collective_id=1, has_side_effects=True, vmem_limit_bytes=40 * 1024 * 1024
        ),
    )(hidden, w, conv_bias[:, :, None])


def group_part(features, voxel_embed, visible, w_query, w_key, w_value):
    width = w_key.shape[0]
    query_data = jnp.einsum(
        "zcxy,cd->zdxy", voxel_embed, w_query, preferred_element_type=jnp.float32
    ).astype(jnp.bfloat16)
    key_data = jnp.einsum(
        "fzcxy,cd->fzdxy", features, w_key, preferred_element_type=jnp.float32
    ).astype(jnp.bfloat16)
    value_data = jnp.einsum(
        "fzcxy,cd->fzdxy", features, w_value, preferred_element_type=jnp.float32
    ).astype(jnp.bfloat16)
    scores = jnp.einsum(
        "zdxy,fzdxy->fzxy", query_data, key_data, preferred_element_type=jnp.float32
    ) / math.sqrt(width)
    is_seen = visible > 0
    highest = jnp.max(jnp.where(is_seen, scores, absent_score), axis=0)
    weights = jnp.where(is_seen, jnp.exp(scores - highest[None]), 0.0)
    weighted = jnp.sum(weights[:, :, None] * value_data, axis=0).astype(jnp.bfloat16)
    totals = jnp.sum(weights, axis=0).astype(jnp.bfloat16)
    return jnp.concatenate([weighted, totals[:, None], highest.astype(jnp.bfloat16)[:, None]], axis=1)


def shards(sizes, features, voxel_embed, visible, w_query, w_key, w_value, w_out, conv_weight, conv_bias):
    width = w_key.shape[0]
    groups = sizes[0]
    planes = features.shape[1] // groups
    me = lax.axis_index("frame")

    def part_for(owner):
        nonlocal features, voxel_embed, visible

        def cut(array, axis):
            return lax.dynamic_slice_in_dim(array, owner * planes, planes, axis)

        return group_part(cut(features, 1), cut(voxel_embed, 0), cut(visible, 1), w_query, w_key, w_value)

    got = []
    for k in range(1, groups):
        part = part_for(lax.rem(me + k, groups))
        part, features, voxel_embed, visible = lax.optimization_barrier((part, features, voxel_embed, visible))
        got.append(lax.ppermute(part, "frame", [(i, (i + k) % groups) for i in range(groups)]))
    got = jnp.stack([part_for(me)] + got)
    got_weighted, got_totals = got[:, :, :width], got[:, :, width]
    got_highest = got[:, :, width + 1].astype(jnp.float32)
    overall = jnp.max(got_highest, axis=0)
    factor = jnp.exp(got_highest - overall[None])
    merged = jnp.sum(factor[:, :, None] * got_weighted.astype(jnp.float32), axis=0)
    norm_sum = jnp.sum(factor * got_totals.astype(jnp.float32), axis=0)
    attended = (merged / norm_sum[:, None]).astype(jnp.bfloat16)
    hidden = jnp.einsum(
        "zcxy,cd->zxdy", attended, w_out, preferred_element_type=jnp.float32
    ).astype(jnp.bfloat16)
    return convs(sizes, hidden, conv_weight, conv_bias).transpose(0, 2, 1, 3)


def solution(mesh):
    sizes = tuple(mesh.shape[a] for a in ("frame", "bx", "by"))
    return jax.shard_map(
        functools.partial(shards, sizes),
        mesh=mesh,
        in_specs=(
            P("frame", None, None, "bx", "by"),
            P(None, None, "bx", "by"),
            P("frame", None, "bx", "by"),
            P(),
            P(),
            P(),
            P(),
            P(),
            P(),
        ),
        out_specs=P("frame", None, "bx", "by"),
        check_vma=False,
    )
```

```python
import functools
import itertools
import math

import jax
import jax.numpy as jnp
from jax import lax
from jax.experimental import pallas as pl
from jax.experimental.pallas import tpu as pltpu
from jax.sharding import PartitionSpec as P

MESH = pl.DeviceIdType.MESH
absent_score = -1e30


def conv_kernel(
    sizes, layers, planes, rows, ch, cols, hid_ref, w_ref, b_ref, out_ref, s3, edge_out, edge_in, partial_sums, send_sem, recv_sem
):
    spots = [lax.axis_index(a) for a in ("frame", "bx", "by")]
    dirs = [
        d
        for d in itertools.product((-1, 0, 1), repeat=3)
        if any(d) and all(k == 0 or n > 1 for k, n in zip(d, sizes))
    ]

    def number(d):
        return (d[0] + 1) * 9 + (d[1] + 1) * 3 + d[2] + 1

    def beside(d):
        found = None
        for k, spot, n in zip(d, spots, sizes):
            if k:
                here = spot > 0 if k < 0 else spot < n - 1
                found = here if found is None else jnp.logical_and(found, here)
        return found

    def device(d):
        return tuple(spot + k for spot, k in zip(spots, d))

    def each(act, some=lambda d: True):
        for d in filter(some, dirs):
            pl.when(beside(d))(functools.partial(act, d))

    def flat(d):
        return d[2] == 0

    def column(d):
        return d[2] != 0

    def straight(d):
        return d[:2] == (0, 0)

    def source(k, length):
        return {-1: pl.ds(1, 1), 0: pl.ds(1, length), 1: pl.ds(length, 1)}[k]

    def halo(k, length):
        return {-1: pl.ds(0, 1), 0: pl.ds(1, length), 1: pl.ds(length + 1, 1)}[k]

    def landing(p, d):
        if d[2] == 0:
            return s3.at[p, halo(d[0], planes), halo(d[1], rows), 1]
        return edge_in.at[p, 0 if d[2] < 0 else 1, d[0] + 1, d[1] + 1]

    def outgoing(p, d):
        if d[2] == 0:
            src = s3.at[p, source(d[0], planes), source(d[1], rows), 1]
        else:
            src = edge_out.at[0 if d[2] < 0 else 1]
        back = tuple(-k for k in d)
        return pltpu.make_async_remote_copy(
            src_ref=src,
            dst_ref=landing(p, back),
            send_sem=send_sem.at[number(d)],
            recv_sem=recv_sem.at[p, number(back)],
            device_id=device(d),
            device_id_type=MESH,
        )

    def incoming(p, d):
        return pltpu.make_async_remote_copy(
            src_ref=landing(p, d),
            dst_ref=landing(p, d),
            send_sem=send_sem.at[number(d)],
            recv_sem=recv_sem.at[p, number(d)],
            device_id=device(d),
            device_id_type=MESH,
        )

    zero = jnp.zeros((ch, cols), jnp.bfloat16)
    for p in range(2):
        for x in range(rows + 2):
            s3[p, 0, x, 1] = zero
            s3[p, planes + 1, x, 1] = zero
        for z in range(1, planes + 1):
            s3[p, z, 0, 1] = zero
            s3[p, z, rows + 1, 1] = zero
        edge_in[p] = jnp.zeros(edge_in.shape[1:], jnp.bfloat16)
    for z in range(planes):
        for x in range(rows):
            s3[0, z + 1, x + 1, 1] = hid_ref[z, x]

    barrier = pltpu.get_barrier_semaphore()
    each(lambda d: pl.semaphore_signal(barrier, inc=1, device_id=device(d), device_id_type=MESH))
    peers = 1
    for spot, n in zip(spots, sizes):
        peers = peers * (1 + (spot > 0).astype(jnp.int32) + (spot < n - 1).astype(jnp.int32))
    pl.semaphore_wait(barrier, peers - 1)

    lane = lax.broadcasted_iota(jnp.int32, (ch, cols), 1)
    pair = 2 if rows % 2 == 0 else 1
    ends = sorted({0, planes - 1})

    def layer(l, carry):
        p = lax.rem(l, 2)

        def pack(z, held):
            low, high = held
            for x in range(rows):
                v = s3[p, z + 1, x + 1, 1]
                j = z * rows + x
                low = jnp.where(lane == j, turned(v, j, 1), low)
                high = jnp.where(lane == j, turned(v, lax.rem(j + 1, cols), 1), high)
            return low, high

        each(lambda d: outgoing(p, d).start(), flat)
        blank = jnp.zeros((ch, cols), jnp.float32)
        low, high = lax.fori_loop(0, planes, pack, (blank, blank))
        edge_out[0] = low.astype(jnp.bfloat16)
        edge_out[1] = high.astype(jnp.bfloat16)
        each(lambda d: outgoing(p, d).start(), straight)
        each(lambda d: outgoing(p, d).start(), lambda d: column(d) and not straight(d))

        def shift(xps, zp, c):
            dz = (zp + planes - 1) // planes
            z = lax.rem(zp + planes - 1, planes)
            for xp in xps:
                dx, x = (xp + rows - 1) // rows, (xp + rows - 1) % rows
                j = z * rows + x
                v = s3[p, zp, xp, 1]
                before = edge_in[p, 0, dz, dx]
                after = edge_in[p, 1, dz, dx]
                left = jnp.where(lane == 0, turned(before, lax.rem(cols - j, cols), 1), turned(v, 1, 1))
                right = jnp.where(
                    lane == cols - 1, turned(after, cols - 1 - j, 1), turned(v, cols - 1, 1)
                )
                s3[p, zp, xp, 0] = left.astype(jnp.bfloat16)
                s3[p, zp, xp, 2] = right.astype(jnp.bfloat16)
            return c

        each(lambda d: incoming(p, d).wait_recv(), straight)
        lax.fori_loop(1, planes + 1, functools.partial(shift, range(1, rows + 1)), 0)
        bias = b_ref[l]

        def product(x0, zp, lo, hi):
            taps = [s3[p, zp, pl.ds(x0 + k, 3)].reshape(9 * ch, cols) for k in range(pair)]
            data = jnp.concatenate(taps, axis=1) if pair > 1 else taps[0]
            return jnp.dot(w_ref[l, lo * ch : (hi + 1) * ch], data, preferred_element_type=jnp.float32)

        def finish(x0, z, total):
            h = total + bias
            h = jnp.where(l < layers - 1, jnp.maximum(h, 0.0), h).astype(jnp.bfloat16)
            for k in range(pair):
                s3[1 - p, z + 1, x0 + 1 + k, 1] = h[:, k * cols : (k + 1) * cols]

        def gather(x0, zps, sums):
            for zp in zps:
                lo, hi = max(0, zp - planes + 1), min(2, zp)
                part = product(x0, zp, lo, hi)
                for a in range(lo, hi + 1):
                    term = part[(a - lo) * ch : (a - lo + 1) * ch]
                    z = zp - a
                    sums[z] = sums[z] + term if z in sums else term
                if zp >= 2 and zp - 2 not in ends:
                    finish(x0, zp - 2, sums.pop(zp - 2))

        def inner_first(i, c):
            sums = {}
            gather(i * pair, range(1, planes + 1), sums)
            for n, z in enumerate(ends):
                partial_sums[i, n] = sums[z]
            return c

        def inner_last(i, c):
            x0 = i * pair
            for n, z in enumerate(ends):
                total = partial_sums[i, n]
                if z == 0:
                    total = total + product(x0, 0, 0, 0)
                if z == planes - 1:
                    total = total + product(x0, planes + 1, 2, 2)
                finish(x0, z, total)
            return c

        def outer(i, c):
            sums = {}
            gather(i * pair, range(planes + 2), sums)
            for z in ends:
                finish(i * pair, z, sums[z])
            return c

        strips = rows // pair
        lax.fori_loop(1, strips - 1, inner_first, 0)
        each(lambda d: incoming(p, d).wait_recv(), lambda d: not straight(d))
        lax.fori_loop(1, planes + 1, functools.partial(shift, (0, rows + 1)), 0)
        lax.fori_loop(0, 2, lambda k, c: shift(range(rows + 2), k * (planes + 1), c), 0)
        lax.fori_loop(1, strips - 1, inner_last, 0)
        edges = min(strips, 2)
        lax.fori_loop(0, edges, lambda k, c: outer(k * (strips - 1), c), 0)
        each(lambda d: outgoing(p, d).wait_send())
        return carry

    lax.fori_loop(0, layers, layer, 0)
    for z in range(planes):
        for x in range(rows):
            out_ref[z, x] = s3[layers % 2, z + 1, x + 1, 1]


def convs(sizes, hidden, conv_weight, conv_bias):
    planes, rows, ch, cols = hidden.shape
    layers = conv_weight.shape[0]
    w = conv_weight.transpose(0, 1, 5, 2, 3, 4).reshape(layers, 3 * ch, 9 * ch)
    whole = pl.BlockSpec(memory_space=pltpu.VMEM)
    return pl.pallas_call(
        functools.partial(conv_kernel, sizes, layers, planes, rows, ch, cols),
        out_shape=jax.ShapeDtypeStruct(hidden.shape, jnp.bfloat16),
        in_specs=[whole] * 3,
        out_specs=whole,
        scratch_shapes=[
            pltpu.VMEM((2, planes + 2, rows + 2, 3, ch, cols), jnp.bfloat16),
            pltpu.VMEM((2, ch, cols), jnp.bfloat16),
            pltpu.VMEM((2, 2, 3, 3, ch, cols), jnp.bfloat16),
            pltpu.VMEM((rows, 2, ch, 2 * cols if rows % 2 == 0 else cols), jnp.float32),
            pltpu.SemaphoreType.DMA((27,)),
            pltpu.SemaphoreType.DMA((2, 27)),
        ],
        compiler_params=pltpu.CompilerParams(
            collective_id=1, has_side_effects=True, vmem_limit_bytes=40 * 1024 * 1024
        ),
    )(hidden, w, conv_bias[:, :, None])


def turned(v, by, axis):
    return pltpu.roll(v, by, axis).astype(jnp.float32)


def group_part(features, voxel_embed, visible, w_query, w_key, w_value):
    width = w_key.shape[0]
    query_data = jnp.einsum(
        "zcxy,cd->zdxy", voxel_embed, w_query, preferred_element_type=jnp.float32
    ).astype(jnp.bfloat16)
    key_data = jnp.einsum(
        "fzcxy,cd->fzdxy", features, w_key, preferred_element_type=jnp.float32
    ).astype(jnp.bfloat16)
    value_data = jnp.einsum(
        "fzcxy,cd->fzdxy", features, w_value, preferred_element_type=jnp.float32
    ).astype(jnp.bfloat16)
    scores = jnp.einsum(
        "zdxy,fzdxy->fzxy", query_data, key_data, preferred_element_type=jnp.float32
    ) / math.sqrt(width)
    is_seen = visible > 0
    highest = jnp.max(jnp.where(is_seen, scores, absent_score), axis=0)
    weights = jnp.where(is_seen, jnp.exp(scores - highest[None]), 0.0)
    weighted = jnp.sum(weights[:, :, None] * value_data, axis=0).astype(jnp.bfloat16)
    totals = jnp.sum(weights, axis=0).astype(jnp.bfloat16)
    return jnp.concatenate([weighted, totals[:, None], highest.astype(jnp.bfloat16)[:, None]], axis=1)


def shards(sizes, features, voxel_embed, visible, w_query, w_key, w_value, w_out, conv_weight, conv_bias):
    width = w_key.shape[0]
    groups = sizes[0]
    planes = features.shape[1] // groups
    me = lax.axis_index("frame")

    def part_for(owner):
        nonlocal w_query, w_key, w_value

        def cut(array, axis):
            return lax.dynamic_slice_in_dim(array, owner * planes, planes, axis)

        return group_part(cut(features, 1), cut(voxel_embed, 0), cut(visible, 1), w_query, w_key, w_value)

    got = []
    for k in range(1, groups):
        part = part_for(lax.rem(me + k, groups))
        part, w_query, w_key, w_value = lax.optimization_barrier((part, w_query, w_key, w_value))
        got.append(lax.ppermute(part, "frame", [(i, (i + k) % groups) for i in range(groups)]))
    got = jnp.stack([part_for(me)] + got)
    got_weighted, got_totals = got[:, :, :width], got[:, :, width]
    got_highest = got[:, :, width + 1].astype(jnp.float32)
    overall = jnp.max(got_highest, axis=0)
    factor = jnp.exp(got_highest - overall[None])
    merged = jnp.sum(factor[:, :, None] * got_weighted.astype(jnp.float32), axis=0)
    norm_sum = jnp.sum(factor * got_totals.astype(jnp.float32), axis=0)
    attended = (merged / norm_sum[:, None]).astype(jnp.bfloat16)
    hidden = jnp.einsum(
        "zcxy,cd->zxdy", attended, w_out, preferred_element_type=jnp.float32
    ).astype(jnp.bfloat16)
    return convs(sizes, hidden, conv_weight, conv_bias).transpose(0, 2, 1, 3)


def solution(mesh):
    sizes = tuple(mesh.shape[a] for a in ("frame", "bx", "by"))
    return jax.shard_map(
        functools.partial(shards, sizes),
        mesh=mesh,
        in_specs=(
            P("frame", None, None, "bx", "by"),
            P(None, None, "bx", "by"),
            P("frame", None, "bx", "by"),
            P(),
            P(),
            P(),
            P(),
            P(),
            P(),
        ),
        out_specs=P("frame", None, "bx", "by"),
        check_vma=False,
    )
```
